32 devices in a mesh: real: 2 (over x), gx: 8 (over z, y), gy: 2 (over core).
Axes of the slice: x: 2, y: 2, z: 4, core: 2. Of those that a mesh axis runs over, the one named last changes fastest.
Arguments:
- conductivity: float32 [3, 64, 128, 256], P(None, 'real', 'gx', 'gy'), parts along dimension 1, may hold values from 0.1 to 10
- part_ids: int32 [64, 128, 256], P('real', 'gx', 'gy'), parts along dimension 0, may hold values from 0 to 255, as said below
- support_mask: int32 [64, 128, 256], P('real', 'gx', 'gy'), parts along dimension 0, may hold values from 0 to 255, as said below
- well_cells: int32 [128], P('real'), parts along dimension 0, may hold values from 0 to 1048575
- well_rates: float32 [128], P('real'), parts along dimension 0, may hold values from 1 to 10
Outputs:
- basis: float32 [8, 64, 128, 256], P(None, 'real', 'gx', 'gy'), parts along dimension 1
- coarse: float32 [8, 16, 4, 8, 8], P('gx', 'gy', 'real'), parts along dimension 2
The draws below stay inside these ranges and needn't reach their ends.
There are 2 independent parts, one for each index of `real`. The reference program is written for one: setup_inputs(seed, part) draws one part's arguments, and reference() takes and returns one part's arrays. A program takes and returns all parts, laid end to end along the dimension named above; each array names one. Nothing has to cross between parts.
Inputs may be any that keep to these rules, and one draw needn't show every extreme that they name: `part_ids`: along each of x, y and z, a cell's block index differs from its coordinate divided by 16 and rounded down by at most one. `support_mask`: bits 0 to 7 only; the bit of the color of the cell's own block is always set.
All inputs are finite; a program needn't handle non-finite values.
Results may differ from the reference program's by a relative error of at most 0.00011.
Values sent between devices are 32-bit elements; how exact they have to be, the bound alone decides.
A program may use at most 192 MiB of HBM per device.

```python
import math
import jax
import jax.numpy as jnp
from jax import lax

NZ = 32
BLOCK = 16
SLOTS = 8
ITERS = 3
NWELL = 64
NX = 128
NY = 256


def partition_helper(key):
    base_key = jax.random.fold_in(key, 7)
    key_x, key_y, key_z = jax.random.split(base_key, 3)
    shift_x = jax.random.randint(key_x, (NZ, 1, NY), -3, 4)
    shift_y = jax.random.randint(key_y, (NZ, NX, 1), -3, 4)
    shift_z = jax.random.randint(key_z, (1, NX, NY), -3, 4)
    coord_z = jnp.arange(NZ, dtype=jnp.int32)[:, None, None]
    coord_x = jnp.arange(NX, dtype=jnp.int32)[None, :, None]
    coord_y = jnp.arange(NY, dtype=jnp.int32)[None, None, :]
    block_x = jnp.clip((coord_x + shift_x) // BLOCK, 0, NX // BLOCK - 1)
    block_y = jnp.clip((coord_y + shift_y) // BLOCK, 0, NY // BLOCK - 1)
    block_z = jnp.clip((coord_z + shift_z) // BLOCK, 0, NZ // BLOCK - 1)
    block_ids = (block_x * (NY // BLOCK) + block_y) * (NZ // BLOCK) + block_z
    return (block_ids.astype(jnp.int32), block_x, block_y, block_z)


def draw_part_ids(key, part):
    return partition_helper(key)[0]


def draw_support_mask(key, part):
    block_ids, block_x, block_y, block_z = partition_helper(key)
    color = block_x % 2 * 4 + block_y % 2 * 2 + block_z % 2
    coord_z = jnp.arange(NZ, dtype=jnp.int32)[:, None, None]
    coord_x = jnp.arange(NX, dtype=jnp.int32)[None, :, None]
    coord_y = jnp.arange(NY, dtype=jnp.int32)[None, None, :]
    mask_key = jax.random.fold_in(key, 29)
    packed = jnp.zeros((NZ, NX, NY), jnp.int32)
    for slot in range(8):
        color_x = slot // 4
        color_y = slot // 2 % 2
        color_z = slot % 2
        slot_keys = jax.random.split(jax.random.fold_in(mask_key, slot), 3)
        jit_x = jax.random.randint(slot_keys[0], (NZ, 1, NY), -2, 3)
        jit_y = jax.random.randint(slot_keys[1], (NZ, NX, 1), -2, 3)
        jit_z = jax.random.randint(slot_keys[2], (1, NX, NY), -2, 3)
        phase_x = (coord_x + jit_x + BLOCK // 2 - color_x * BLOCK) % (2 * BLOCK)
        phase_y = (coord_y + jit_y + BLOCK // 2 - color_y * BLOCK) % (2 * BLOCK)
        phase_z = (coord_z + jit_z + BLOCK // 2 - color_z * BLOCK) % (2 * BLOCK)
        inside_x = (phase_x >= 2) & (phase_x < 2 * BLOCK - 2)
        inside_y = (phase_y >= 2) & (phase_y < 2 * BLOCK - 2)
        inside_z = (phase_z >= 2) & (phase_z < 2 * BLOCK - 2)
        member = inside_x & inside_y & inside_z | (color == slot)
        packed = packed + member.astype(jnp.int32) * 2 ** slot
    return packed


def plant(array, key, least, top_value):
    dims = array.shape
    index_at = [jax.random.randint(jax.random.fold_in(key, axis), (), 0, dims[axis]) for axis in range(len(dims))]
    array = array.at[tuple(index_at)].set(least)
    longest = dims.index(max(dims))
    index_at[longest] = (index_at[longest] + 1) % dims[longest]
    return array.at[tuple(index_at)].set(top_value)


def block_levels(own_key, extent, cuts, smallest, largest):
    gain, own = 1.0, jax.random.fold_in(own_key, 6)
    for axis_at, shards_of in cuts:
        steps = jnp.exp(jax.random.uniform(jax.random.fold_in(own, axis_at), (shards_of,), jnp.float32, smallest / len(cuts), largest / len(cuts)))
        gain = gain * jnp.repeat(steps, extent[axis_at] // shards_of).reshape([-1 if axis == axis_at else 1 for axis in range(len(extent))])
    return gain


def setup_inputs(seed: int = 0, part: int = 0) -> dict:
    seeds = jax.random.split(jax.random.key(seed), 6)
    part_keys = jax.random.split(jax.random.fold_in(seeds[5], part), 6)
    return {
        "conductivity": jnp.clip(jnp.exp(math.log(10.0) - 4.6051702 * jax.random.uniform(part_keys[0], (3, NZ, NX, NY), jnp.float32) ** block_levels(part_keys[0], (3, NZ, NX, NY), ((2, 8), (3, 2)), -0.2, 0.2)), 0.1, 10.0),
        "part_ids": draw_part_ids(jax.random.fold_in(jax.random.fold_in(seeds[5], part), 71), part),
        "support_mask": draw_support_mask(jax.random.fold_in(jax.random.fold_in(seeds[5], part), 71), part),
        "well_cells": plant(jax.random.randint(part_keys[3], (NWELL,), 0, NZ * NX * NY), jax.random.fold_in(part_keys[3], 1), 0, (NZ * NX * NY) - 1).astype(jnp.int32),
        "well_rates": jnp.clip(jnp.exp(jax.random.uniform(part_keys[4], (NWELL,), jnp.float32, math.log(1.0), math.log(10.0))), 1.0, 10.0),
    }


relax_weight = 2.0 / 3.0


def transmit(near_cond, far_cond):
    return 2.0 * near_cond * far_cond / (near_cond + far_cond)


def pad_axis(values, axis, before, after):
    widths = [(0, 0)] * values.ndim
    widths[axis] = (before, after)
    return jnp.pad(values, widths)


def operate(basis, cond, well_field):
    flow_x = transmit(cond[0][:, :-1], cond[0][:, 1:])
    flow_y = transmit(cond[1][:, :, :-1], cond[1][:, :, 1:])
    flow_z = transmit(cond[2][:-1], cond[2][1:])
    diff_x = flow_x * (basis[:, :, 1:] - basis[:, :, :-1])
    diff_y = flow_y * (basis[:, :, :, 1:] - basis[:, :, :, :-1])
    diff_z = flow_z * (basis[:, 1:] - basis[:, :-1])
    applied = well_field * basis
    applied = applied - pad_axis(diff_x, 2, 0, 1) + pad_axis(diff_x, 2, 1, 0)
    applied = applied - pad_axis(diff_y, 3, 0, 1) + pad_axis(diff_y, 3, 1, 0)
    applied = applied - pad_axis(diff_z, 1, 0, 1) + pad_axis(diff_z, 1, 1, 0)
    diagonal = well_field + pad_axis(flow_x, 1, 0, 1) + pad_axis(flow_x, 1, 1, 0)
    diagonal = diagonal + pad_axis(flow_y, 2, 0, 1) + pad_axis(flow_y, 2, 1, 0)
    diagonal = diagonal + pad_axis(flow_z, 0, 0, 1) + pad_axis(flow_z, 0, 1, 0)
    return applied, diagonal


def reference(conductivity, part_ids, support_mask, well_cells, well_rates):
    blocks_x = NX // BLOCK
    blocks_y = NY // BLOCK
    blocks_z = NZ // BLOCK
    cell_count = NZ * NX * NY
    well_field = jnp.zeros((cell_count,), jnp.float32).at[well_cells].add(well_rates).reshape(NZ, NX, NY)
    block_x = part_ids // (blocks_y * blocks_z)
    block_y = (part_ids // blocks_z) % blocks_y
    block_z = part_ids % blocks_z
    color = (block_x % 2) * 4 + (block_y % 2) * 2 + block_z % 2
    slot_ids = jnp.arange(SLOTS, dtype=jnp.int32)[:, None, None, None]
    basis = (color[None] == slot_ids).astype(jnp.float32)
    allowed = jnp.bitwise_and(jnp.right_shift(support_mask[None], slot_ids), 1).astype(jnp.float32)
    for sweep in range(ITERS):
        applied, diagonal = operate(basis, conductivity, well_field)
        basis = allowed * (basis - relax_weight * applied / diagonal)
    applied, diagonal = operate(basis, conductivity, well_field)

    def per_layer(running, pieces):
        basis_layer, applied_layer, ids_layer = pieces
        outer = (basis_layer[:, None] * applied_layer[None]).reshape(SLOTS * SLOTS, -1).T
        added = jax.ops.segment_sum(outer, ids_layer.reshape(-1), num_segments=blocks_x * blocks_y * blocks_z)
        return running + added, None

    start_sum = jnp.zeros((blocks_x * blocks_y * blocks_z, SLOTS * SLOTS), jnp.float32)
    coarse, unused = lax.scan(per_layer, start_sum, (jnp.transpose(basis, (1, 0, 2, 3)), jnp.transpose(applied, (1, 0, 2, 3)), part_ids))
    return basis, coarse.reshape(blocks_x, blocks_y, blocks_z, SLOTS, SLOTS)
```

```python
import jax
import jax.numpy as jnp
from jax import lax
from jax.experimental import pallas as pl
from jax.experimental.pallas import tpu as pltpu
from jax.sharding import PartitionSpec as P

NZ = 32
BLOCK = 16
SLOTS = 8
ITERS = 3
SX = 16
LY = 128
REACH = ITERS + 1
EXT = 32
TOP = 8
RB = SX + 2 * REACH
VMEM = pl.BlockSpec(memory_space=pltpu.VMEM)
RELAX = 2.0 / 3.0


def colour_of(ids):
    bx = lax.shift_right_logical(ids, 5)
    by = lax.shift_right_logical(ids, 1)
    return (bx & 1) * 4 + (by & 1) * 2 + (ids & 1)


def pack_window(get, rows):
    lane = lax.broadcasted_iota(jnp.int32, (rows, LY), 1)
    halves = []
    for zh in range(2):
        total = jnp.zeros((rows, LY), jnp.float32)
        for zl in range(16):
            moved = pltpu.roll(get(zh * 16 + zl), 8 * zl + 4, 1)
            total = jnp.where(lax.shift_right_logical(lane, 3) == zl, moved, total)
        halves.append(total)
    return halves


def pack_kernel(cond, part, mask, to_prev, to_next, mini, mini_prev, mini_next, fields):
    for f in range(3):
        fields[f] = cond[f]
    fields[3] = colour_of(part[...]).astype(jnp.float32)
    fields[4] = mask[...].astype(jnp.float32)
    to_prev[...] = fields[:, :, 0:REACH, :]
    to_next[...] = fields[:, :, SX - REACH : SX, :]
    for f in range(5):
        halves = pack_window(lambda z: fields[f, z], SX)
        for zh in range(2):
            mini[f, zh] = halves[zh]
            mini_prev[f, zh] = halves[zh][0:REACH]
            mini_next[f, zh] = halves[zh][SX - REACH : SX]


def transmit(near, far):
    total = near + far
    good = total > 0
    return jnp.where(good, 2.0 * near * far / jnp.where(good, total, 1.0), 0.0)


def main_kernel(
    cond, part, mask, above, below, mini_own, mini_y, mini_above, mini_below, wells, rates,
    out, acc,
    field, coef, diag, well_main, q_class, y_class, b0, b1,
    mfield, mcoef, mbasis, lhs, rhs, ints,
):
    gx = lax.axis_index("gx")
    gy = lax.axis_index("gy")
    ngx = lax.axis_size("gx")
    f32 = jnp.float32
    lane = lax.broadcasted_iota(jnp.int32, (EXT, LY), 1)
    zero_tile = jnp.zeros((EXT, LY), f32)

    def fill(z, carry):
        base = pl.multiple_of(z * EXT, EXT)
        own = pl.multiple_of(z * EXT + TOP, 8)
        for f in range(5):
            field[f, pl.ds(base, 8), :] = zero_tile[:8]
            field[f, pl.ds(base + 24, 8), :] = zero_tile[:8]
        ids = part[z]
        for f in range(3):
            field[f, pl.ds(own, SX), :] = cond[f, z]
        field[3, pl.ds(own, SX), :] = colour_of(ids).astype(f32)
        field[4, pl.ds(own, SX), :] = mask[z].astype(f32)
        for f in range(5):
            field[f, pl.ds(base + 4, 4), :] = above[f, z]
            field[f, pl.ds(base + 24, 4), :] = below[f, z]
        row = pl.multiple_of(z * SX, SX)
        bx = lax.shift_right_logical(ids, 5) - gx + 1
        by = (lax.shift_right_logical(ids, 1) & 15) - gy * 8 + 1
        q_class[pl.ds(row, SX), :] = (bx * 2 + (ids & 1)).astype(f32)
        y_class[pl.ds(row, SX), :] = by.astype(f32)
        ints[pl.ds(base, EXT), :] = field[4, pl.ds(base, EXT), :].astype(jnp.int32)
        return carry

    lax.fori_loop(0, NZ, fill, 0)

    side = lax.shift_right_logical(lane, 2) & 1
    for f in range(5):
        up = pack_window(lambda z: above[f, z], REACH)
        dn = pack_window(lambda z: below[f, z], REACH)
        for zh in range(2):
            at = zh * EXT
            mfield[f, at : at + 8, :] = zero_tile[:8]
            mfield[f, at + 24 : at + 32, :] = zero_tile[:8]
            mine4 = side[:REACH] == gy
            mfield[f, at + 4 : at + 8, :] = jnp.where(mine4, up[zh], mini_above[f, zh])
            mfield[f, at + 24 : at + 28, :] = jnp.where(mine4, dn[zh], mini_below[f, zh])
            mfield[f, at + 8 : at + 24, :] = jnp.where(
                side[:SX] == gy, mini_own[f, zh], mini_y[f, zh]
            )

    cells = wells[...]
    place_y = cells & 255
    place_x = lax.shift_right_logical(cells, 8) & (SX * ngx - 1)
    place_z = lax.shift_right_logical(cells, 8 + (SX * ngx).bit_length() - 1)
    row_x = place_x - gx * SX + TOP
    inside_x = (row_x >= 4) & (row_x < 28)
    nw = cells.shape[1]

    def spread(rows, row_of, lane_of, ok):
        at_row = lax.broadcasted_iota(jnp.int32, (rows, nw), 0)
        hot = jnp.where((at_row == row_of) & ok, 1.0, 0.0).astype(f32)
        at_lane = lax.broadcasted_iota(jnp.int32, (LY, nw), 0)
        val = jnp.where(at_lane == lane_of, rates[...], 0.0)
        return lax.dot_general(
            hot, val, (((1,), (1,)), ((), ())),
            precision=lax.Precision.HIGHEST, preferred_element_type=f32,
        )

    own_y = place_y - gy * LY
    well_main[...] = spread(
        NZ * EXT, place_z * EXT + row_x, own_y, inside_x & (own_y >= 0) & (own_y < LY)
    )
    col = place_y - (LY - 4)
    well_mini = spread(
        2 * EXT,
        lax.shift_right_logical(place_z, 4) * EXT + row_x,
        (place_z & 15) * 8 + col,
        inside_x & (col >= 0) & (col < 8),
    )

    def finish(flows, well):
        total = well + flows[0] + flows[1] + flows[2] + flows[3] + flows[4] + flows[5]
        total = jnp.where(total > 0, total, 1.0)
        scale = RELAX / total
        return total, [flow * scale for flow in flows]

    for zh in range(2):
        at = zh * EXT
        kx, ky, kz = (mfield[f, at : at + EXT, :] for f in range(3))
        other = mfield[2, (1 - zh) * EXT : (2 - zh) * EXT, :]
        xp = transmit(kx, pltpu.roll(kx, EXT - 1, 0))
        xm = pltpu.roll(xp, 1, 0)
        yp = transmit(ky, pltpu.roll(ky, LY - 1, 1))
        ym = pltpu.roll(yp, 1, 1)
        up = pltpu.roll(kz, LY - 8, 1)
        dn = pltpu.roll(kz, 8, 1)
        if zh == 0:
            up = jnp.where(lane < LY - 8, up, pltpu.roll(other, LY - 8, 1))
            zp = transmit(kz, up)
            zm = jnp.where(lane < 8, 0.0, transmit(kz, dn))
        else:
            dn = jnp.where(lane >= 8, dn, pltpu.roll(other, 8, 1))
            zp = jnp.where(lane < LY - 8, transmit(kz, up), 0.0)
            zm = transmit(kz, dn)
        unused, parts = finish((xm, xp, ym, yp, zm, zp), well_mini[at : at + EXT])
        for d in range(6):
            mcoef[d, at : at + EXT, :] = parts[d]

    def shift_of(z):
        return 123 + 2 * gy - 8 * (z & 15)

    def coefs(z, zm):
        base = pl.multiple_of(z * EXT, EXT)
        here = pl.ds(base, EXT)
        kx, ky, kz = (field[f, here, :] for f in range(3))
        half = pl.multiple_of(lax.shift_right_logical(z, 4) * EXT, EXT)
        edge = pltpu.roll(mfield[1, pl.ds(half, EXT), :], shift_of(z), 1)
        xp = transmit(kx, pltpu.roll(kx, EXT - 1, 0))
        xm = pltpu.roll(xp, 1, 0)
        yp = transmit(ky, jnp.where(lane == LY - 1, edge, pltpu.roll(ky, LY - 1, 1)))
        yp = jnp.where((lane == LY - 1) & (gy == 1), 0.0, yp)
        first = jnp.where(gy == 1, transmit(ky, edge), 0.0)
        ym = jnp.where(lane == 0, first, pltpu.roll(yp, 1, 1))
        later = pl.multiple_of(jnp.minimum(z + 1, NZ - 1) * EXT, EXT)
        zp = transmit(kz, field[2, pl.ds(later, EXT), :])
        zp = jnp.where(z == NZ - 1, 0.0, zp)
        total, parts = finish((xm, xp, ym, yp, zm, zp), well_main[here, :])
        diag[here, :] = total
        for d in range(6):
            coef[d, here, :] = parts[d]
        return zp

    lax.fori_loop(0, NZ, coefs, zero_tile)

    slot = lax.broadcasted_iota(jnp.int32, (SLOTS, LY), 0)
    slot_f = slot.astype(f32)
    bit = lax.shift_left(jnp.ones_like(slot), slot)
    lane8 = lax.broadcasted_iota(jnp.int32, (SLOTS, LY), 1)
    is_last = lane8 == LY - 1
    is_first = lane8 == 0
    zero8 = jnp.zeros((SLOTS, LY), f32)

    def wide(ref, row):
        return jnp.broadcast_to(ref[pl.ds(row, 1), :], (SLOTS, LY))

    for zh in range(2):
        for s in range(RB):
            mbasis[0, zh, s] = (wide(mfield.at[3], zh * EXT + 4 + s) == slot_f).astype(f32)
    for it in range(ITERS):
        mbasis[it + 1] = jnp.zeros((2, RB, SLOTS, LY), f32)

        def window(s, carry):
            both = (mbasis[it, 0, s], mbasis[it, 1, s])
            ups = [pltpu.roll(v, LY - 8, 1) for v in both]
            dns = [pltpu.roll(v, 8, 1) for v in both]
            ups[0] = jnp.where(lane8 < LY - 8, ups[0], ups[1])
            dns[1] = jnp.where(lane8 >= 8, dns[1], dns[0])
            for zh in range(2):
                row = zh * EXT + 4 + s
                value = both[zh]
                near = (
                    mbasis[it, zh, s - 1], mbasis[it, zh, s + 1],
                    pltpu.roll(value, 1, 1), pltpu.roll(value, LY - 1, 1),
                    dns[zh], ups[zh],
                )
                new = (1.0 - RELAX) * value
                for d in range(6):
                    new = new + wide(mcoef.at[d], row) * near[d]
                bits = wide(mfield.at[4], row).astype(jnp.int32) & bit
                mbasis[it + 1, zh, s] = jnp.where(bits != 0, new, 0.0)
            return carry

        lax.fori_loop(it + 1, RB - it - 1, window, 0)

    for ref in (b0, b1):
        ref[0] = jnp.zeros((RB, SLOTS, LY), f32)
        ref[NZ + 1] = jnp.zeros((RB, SLOTS, LY), f32)

    def start(z, carry):
        for s in range(RB):
            b0[z + 1, s] = (wide(field.at[3], z * EXT + 4 + s) == slot_f).astype(f32)
        return carry

    lax.fori_loop(0, NZ, start, 0)

    def spread_sum(src, it, z, s, before, value, after):
        row = z * EXT + 4 + s
        edge = pltpu.roll(mbasis[it, lax.shift_right_logical(z, 4), s], shift_of(z), 1)
        left = jnp.where(is_first, edge, pltpu.roll(value, 1, 1))
        right = jnp.where(is_last, edge, pltpu.roll(value, LY - 1, 1))
        near = (before, after, left, right, src[z, s], src[z + 2, s])
        terms = [wide(coef.at[d], row) * near[d] for d in range(6)]
        return (terms[0] + terms[1]) + (terms[2] + terms[3]) + (terms[4] + terms[5])

    for it in range(ITERS):
        src, dst = ((b0, b1), (b1, b0))[it % 2]

        def smooth(z, carry):
            before = src[z + 1, it]
            value = src[z + 1, it + 1]
            for s in range(it + 1, RB - it - 1):
                after = src[z + 1, s + 1]
                new = (1.0 - RELAX) * value + spread_sum(src, it, z, s, before, value, after)
                bits = wide(ints, z * EXT + 4 + s) & bit
                dst[z + 1, s] = jnp.where(bits != 0, new, 0.0)
                before, value = value, after
            return carry

        lax.fori_loop(0, NZ, smooth, 0)

    src = (b0, b1)[ITERS % 2]
    acc[...] = jnp.zeros_like(acc)

    def both_parts(value):
        high = value.astype(jnp.bfloat16).astype(f32)
        return high, value - high

    def gather(z, carry):
        before = src[z + 1, REACH - 1]
        value = src[z + 1, REACH]
        for x in range(SX):
            s = x + REACH
            after = src[z + 1, s + 1]
            total = spread_sum(src, ITERS, z, s, before, value, after)
            applied = wide(diag, z * EXT + 4 + s) * (value - 1.5 * total)
            out[pl.ds(z * SX + x, SLOTS, stride=NZ * SX), :] = value
            at = slice(x * LY, (x + 1) * LY)
            q = wide(q_class, z * SX + x)
            y = wide(y_class, z * SX + x)
            bh, bl = both_parts(value)
            ah, al = both_parts(applied)
            for c in range(6):
                hit = q == float(c)
                pair = jnp.concatenate([jnp.where(hit, bh, zero8), jnp.where(hit, bl, zero8)], 0)
                lhs[c * 16 : c * 16 + 16, at] = pair.astype(jnp.bfloat16)
            for c in range(10):
                hit = y == float(c)
                pair = jnp.concatenate([jnp.where(hit, ah, zero8), jnp.where(hit, al, zero8)], 0)
                rhs[c * 16 : c * 16 + 16, at] = pair.astype(jnp.bfloat16)
            before, value = value, after
        acc[...] += lax.dot_general(
            lhs[...], rhs[...], (((1,), (1,)), ((), ())), preferred_element_type=f32
        )
        return carry

    lax.fori_loop(0, NZ, gather, 0)


def body(conductivity, part_ids, support_mask, well_cells, well_rates):
    f32 = jnp.float32
    count = lax.axis_size("gx")
    shape = jax.ShapeDtypeStruct
    to_prev, to_next, mini, mini_prev, mini_next = pl.pallas_call(
        pack_kernel,
        out_shape=(
            shape((5, NZ, REACH, LY), f32),
            shape((5, NZ, REACH, LY), f32),
            shape((5, 2, SX, LY), f32),
            shape((5, 2, REACH, LY), f32),
            shape((5, 2, REACH, LY), f32),
        ),
        in_specs=[VMEM] * 3,
        out_specs=(VMEM,) * 5,
        scratch_shapes=[pltpu.VMEM((5, NZ, SX, LY), f32)],
        compiler_params=pltpu.CompilerParams(vmem_limit_bytes=32 * 2**20),
        name="pack",
    )(conductivity, part_ids, support_mask)
    down = [(i, i + 1) for i in range(count - 1)]
    up = [(i + 1, i) for i in range(count - 1)]
    flip = [(0, 1), (1, 0)]

    def cross(pairs):
        return [(a * 2 + c, b * 2 + 1 - c) for a, b in pairs for c in range(2)]

    above = lax.ppermute(to_next, "gx", down)
    below = lax.ppermute(to_prev, "gx", up)
    mini_y = lax.ppermute(mini, "gy", flip)
    mini_above = lax.ppermute(mini_next, ("gx", "gy"), cross(down))
    mini_below = lax.ppermute(mini_prev, ("gx", "gy"), cross(up))
    basis, acc = pl.pallas_call(
        main_kernel,
        out_shape=(shape((SLOTS * NZ * SX, LY), f32), shape((96, 160), f32)),
        in_specs=[VMEM] * 11,
        out_specs=(VMEM,) * 2,
        scratch_shapes=[
            pltpu.VMEM((5, NZ * EXT, LY), f32),
            pltpu.VMEM((6, NZ * EXT, LY), f32),
            pltpu.VMEM((NZ * EXT, LY), f32),
            pltpu.VMEM((NZ * EXT, LY), f32),
            pltpu.VMEM((NZ * SX, LY), f32),
            pltpu.VMEM((NZ * SX, LY), f32),
            pltpu.VMEM((NZ + 2, RB, SLOTS, LY), f32),
            pltpu.VMEM((NZ + 2, RB, SLOTS, LY), f32),
            pltpu.VMEM((5, 2 * EXT, LY), f32),
            pltpu.VMEM((6, 2 * EXT, LY), f32),
            pltpu.VMEM((ITERS + 1, 2, RB, SLOTS, LY), f32),
            pltpu.VMEM((96, SX * LY), jnp.bfloat16),
            pltpu.VMEM((160, SX * LY), jnp.bfloat16),
            pltpu.VMEM((NZ * EXT, LY), jnp.int32),
        ],
        compiler_params=pltpu.CompilerParams(vmem_limit_bytes=48 * 2**20),
        name="smooth",
    )(
        conductivity, part_ids, support_mask, above, below, mini, mini_y, mini_above, mini_below,
        well_cells.reshape(1, -1), well_rates.reshape(1, -1),
    )
    sums = acc.reshape(3, 2, 2, SLOTS, 10, 2, SLOTS).sum((2, 5))
    grid = jnp.transpose(sums, (0, 3, 1, 2, 4)).reshape(3, 10, 2, SLOTS * SLOTS)
    from_above = lax.ppermute(grid[:, 0], "gy", [(1, 0)])
    from_below = lax.ppermute(grid[:, 9], "gy", [(0, 1)])
    grid = grid.at[:, 8].add(from_above).at[:, 1].add(from_below)
    from_right = lax.ppermute(grid[0], "gx", up)
    from_left = lax.ppermute(grid[2], "gx", down)
    total = (grid[1] + from_right + from_left)[1:9]
    return (
        basis.reshape(SLOTS, NZ, SX, LY),
        total.reshape(1, 8, 2, SLOTS, SLOTS),
    )


def solution(mesh):
    placed = (
        P(None, "real", "gx", "gy"),
        P("real", "gx", "gy"),
        P("real", "gx", "gy"),
        P("real"),
        P("real"),
    )
    return jax.shard_map(
        body,
        mesh=mesh,
        in_specs=placed,
        out_specs=(P(None, "real", "gx", "gy"), P("gx", "gy", "real", None, None)),
        check_vma=False,
    )
```

```python
import jax
import jax.numpy as jnp
from jax import lax
from jax.experimental import pallas as pl
from jax.experimental.pallas import tpu as pltpu
from jax.sharding import PartitionSpec as P

NZ = 32
BLOCK = 16
SLOTS = 8
ITERS = 3
SX = 16
LY = 128
REACH = ITERS + 1
EXT = 32
TOP = 8
RB = SX + 2 * REACH
VMEM = pl.BlockSpec(memory_space=pltpu.VMEM)
RELAX = 2.0 / 3.0


def colour_of(ids):
    bx = lax.shift_right_logical(ids, 5)
    by = lax.shift_right_logical(ids, 1)
    return (bx & 1) * 4 + (by & 1) * 2 + (ids & 1)


def pack_window(get, rows):
    lane = lax.broadcasted_iota(jnp.int32, (rows, LY), 1)
    halves = []
    for zh in range(2):
        total = jnp.zeros((rows, LY), jnp.float32)
        for zl in range(16):
            moved = pltpu.roll(get(zh * 16 + zl), 8 * zl + 4, 1)
            total = jnp.where(lax.shift_right_logical(lane, 3) == zl, moved, total)
        halves.append(total)
    return halves


FROM_PREV = [
    (f, SX - REACH + i, TOP - REACH + i)
    for i in range(REACH)
    for f in ((0, 3) if i == 0 else range(5))
]
FROM_NEXT = [
    (f, i, TOP + SX + i) for i in range(REACH) for f in ((0, 3) if i == REACH - 1 else range(5))
]
PLANES = len(FROM_PREV)


def others(gx, gy, ngx):
    return (
        (gx < ngx - 1, {"gx": gx + 1, "gy": gy}),
        (gx > 0, {"gx": gx - 1, "gy": gy}),
        (None, {"gx": gx, "gy": 1 - gy}),
        (gx < ngx - 1, {"gx": gx + 1, "gy": 1 - gy}),
        (gx > 0, {"gx": gx - 1, "gy": 1 - gy}),
    )


def guarded(condition, action):
    if condition is None:
        action()
    else:
        pl.when(condition)(action)


def greet(targets):
    barrier = pltpu.get_barrier_semaphore()
    for condition, device in targets:
        guarded(condition, lambda: pl.semaphore_signal(
            barrier, inc=1, device_id=device, device_id_type=pl.DeviceIdType.MESH))
    ahead = jnp.minimum(lax.axis_size("gx") - 1 - lax.axis_index("gx"), 1)
    pl.semaphore_wait(barrier, 1 + 2 * ahead + 2 * jnp.minimum(lax.axis_index("gx"), 1))


def exchange_kernel(
    cond, part, mask, mini, above, below, mini_y, mini_above, mini_below,
    fields, part_in, mask_in, to_prev, to_next, mini_prev, mini_next, load_sem, send_sem, recv_sem,
):
    gx = lax.axis_index("gx")
    gy = lax.axis_index("gy")
    targets = others(gx, gy, lax.axis_size("gx"))
    loads = [
        pltpu.make_async_copy(cond, fields.at[0:3], load_sem.at[0]),
        pltpu.make_async_copy(part, part_in, load_sem.at[1]),
        pltpu.make_async_copy(mask, mask_in, load_sem.at[2]),
    ]
    for load in loads:
        load.start()
    has_source = (gx > 0, gx < lax.axis_size("gx") - 1)
    for ref, source in ((above, 0), (below, 1), (mini_above, 0), (mini_below, 1)):
        @pl.when(jnp.logical_not(has_source[source]))
        def _():
            ref[...] = jnp.zeros_like(ref)

    for load in loads:
        load.wait()
    fields[3] = colour_of(part_in[...]).astype(jnp.float32)
    fields[4] = mask_in[...].astype(jnp.float32)
    for n, (f, row, unused) in enumerate(FROM_NEXT):
        to_prev[n] = fields[f, pl.ds(row, NZ, stride=SX), :]
    for n, (f, row, unused) in enumerate(FROM_PREV):
        to_next[n] = fields[f, pl.ds(row, NZ, stride=SX), :]
    pairs = (
        (to_next, above), (to_prev, below), (mini, mini_y),
        (mini_next, mini_above), (mini_prev, mini_below),
    )
    copies = [
        pltpu.make_async_remote_copy(
            src_ref=src, dst_ref=dst, send_sem=send_sem.at[n], recv_sem=recv_sem.at[n],
            device_id=targets[n][1], device_id_type=pl.DeviceIdType.MESH,
        )
        for n, (src, dst) in enumerate(pairs)
    ]
    greet(targets)
    for n in (0, 1):
        guarded(targets[n][0], copies[n].start)
    for f in range(5):
        halves = pack_window(lambda z: fields[f, z * SX : z * SX + SX], SX)
        for zh in range(2):
            mini[f, zh] = halves[zh]
            mini_prev[f, zh] = halves[zh][0:REACH]
            mini_next[f, zh] = halves[zh][SX - REACH : SX]
    for n in (2, 3, 4):
        guarded(targets[n][0], copies[n].start)
    sources = (has_source[0], has_source[1], None, has_source[0], has_source[1])
    for n in range(5):
        guarded(targets[n][0], copies[n].wait_send)
        guarded(sources[n], copies[n].wait_recv)


def total_kernel(acc, out, grid, edge, from_prev, from_next, edge_y, edge_prev, edge_next,
                 send_sem, recv_sem):
    gx = lax.axis_index("gx")
    gy = lax.axis_index("gy")
    ngx = lax.axis_size("gx")
    targets = others(gx, gy, ngx)
    has_source = (gx > 0, gx < ngx - 1)
    for ref, source in ((from_prev, 0), (from_next, 1), (edge_prev, 0), (edge_next, 1)):
        @pl.when(jnp.logical_not(has_source[source]))
        def _():
            ref[...] = jnp.zeros_like(ref)

    for y in range(10):
        both = acc[y * 16 : y * 16 + 8] + acc[y * 16 + 8 : y * 16 + 16]
        grid[y * 8 : y * 8 + 8] = both + pltpu.roll(both, LY - 8, 1)
    edge[...] = jnp.where(gy == 1, grid[0:8], grid[72:80])
    pairs = ((grid, from_prev), (grid, from_next), (edge, edge_y), (edge, edge_prev), (edge, edge_next))
    copies = [
        pltpu.make_async_remote_copy(
            src_ref=src, dst_ref=dst, send_sem=send_sem.at[n], recv_sem=recv_sem.at[n],
            device_id=targets[n][1], device_id_type=pl.DeviceIdType.MESH,
        )
        for n, (src, dst) in enumerate(pairs)
    ]
    greet(targets)
    sources = (has_source[0], has_source[1], None, has_source[0], has_source[1])
    for n in range(5):
        guarded(targets[n][0], copies[n].start)
    for n in range(5):
        guarded(targets[n][0], copies[n].wait_send)
        guarded(sources[n], copies[n].wait_recv)
    for y in range(8):
        at = slice(y * 8 + 8, y * 8 + 16)
        mid, prev, after = grid[at], from_prev[at], from_next[at]
        if y in (0, 7):
            use = gy == (0 if y == 7 else 1)
            mid = mid + jnp.where(use, edge_y[...], 0.0)
            prev = prev + jnp.where(use, edge_prev[...], 0.0)
            after = after + jnp.where(use, edge_next[...], 0.0)
        out[y * 8 : y * 8 + 8] = (
            pltpu.roll(mid, LY - 32, 1) + after + pltpu.roll(prev, LY - 64, 1)
        )


def transmit(near, far):
    total = near + far
    good = total > 0
    return jnp.where(good, 2.0 * near * far / jnp.where(good, total, 1.0), 0.0)


def main_kernel(
    cond_hbm, part_hbm, mask_hbm, above, below, mini_own, mini_y, mini_above, mini_below, wells, rates,
    out, acc,
    field, coef, diag, well_main, q_class, y_class, b0, b1,
    mfield, mcoef, mbasis, lhs, rhs, ints, cond, part, mask, load_sem,
):
    loads = [
        pltpu.make_async_copy(src, dst, load_sem.at[n])
        for n, (src, dst) in enumerate(((cond_hbm, cond), (part_hbm, part), (mask_hbm, mask)))
    ]
    for load in loads:
        load.start()
    for load in loads:
        load.wait()
    gx = lax.axis_index("gx")
    gy = lax.axis_index("gy")
    ngx = lax.axis_size("gx")
    f32 = jnp.float32
    lane = lax.broadcasted_iota(jnp.int32, (EXT, LY), 1)
    zero_tile = jnp.zeros((EXT, LY), f32)

    def fill(z, carry):
        base = pl.multiple_of(z * EXT, EXT)
        own = pl.multiple_of(z * EXT + TOP, 8)
        for f in range(5):
            field[f, pl.ds(base, 8), :] = zero_tile[:8]
            field[f, pl.ds(base + 24, 8), :] = zero_tile[:8]
        row = pl.multiple_of(z * SX, SX)
        ids = part[pl.ds(row, SX), :]
        for f in range(3):
            field[f, pl.ds(own, SX), :] = cond[f, pl.ds(row, SX), :]
        field[3, pl.ds(own, SX), :] = colour_of(ids).astype(f32)
        field[4, pl.ds(own, SX), :] = mask[pl.ds(row, SX), :].astype(f32)
        bx = lax.shift_right_logical(ids, 5) - gx + 1
        by = (lax.shift_right_logical(ids, 1) & 15) - gy * 8 + 1
        q_class[pl.ds(row, SX), :] = (bx * 2 + (ids & 1)).astype(f32)
        y_class[pl.ds(row, SX), :] = by.astype(f32)
        ints[pl.ds(base, 8), :] = jnp.zeros((8, LY), jnp.int32)
        ints[pl.ds(base + 24, 8), :] = jnp.zeros((8, LY), jnp.int32)
        ints[pl.ds(own, SX), :] = mask[pl.ds(row, SX), :]
        return carry

    lax.fori_loop(0, NZ, fill, 0)
    for planes, ref in ((FROM_PREV, above), (FROM_NEXT, below)):
        for n, (f, unused, row) in enumerate(planes):
            field[f, pl.ds(row, NZ, stride=EXT), :] = ref[n]
            if f == 4:
                ints[pl.ds(row, NZ, stride=EXT), :] = ref[n].astype(jnp.int32)

    side = lax.shift_right_logical(lane, 2) & 1
    for f in range(5):
        up = pack_window(lambda z: field[f, z * EXT + 4 : z * EXT + 8], REACH)
        dn = pack_window(lambda z: field[f, z * EXT + 24 : z * EXT + 28], REACH)
        for zh in range(2):
            at = zh * EXT
            mfield[f, at : at + 8, :] = zero_tile[:8]
            mfield[f, at + 24 : at + 32, :] = zero_tile[:8]
            mine4 = side[:REACH] == gy
            mfield[f, at + 4 : at + 8, :] = jnp.where(mine4, up[zh], mini_above[f, zh])
            mfield[f, at + 24 : at + 28, :] = jnp.where(mine4, dn[zh], mini_below[f, zh])
            mfield[f, at + 8 : at + 24, :] = jnp.where(
                side[:SX] == gy, mini_own[f, zh], mini_y[f, zh]
            )

    cells = wells[...]
    place_y = cells & 255
    place_x = lax.shift_right_logical(cells, 8) & (SX * ngx - 1)
    place_z = lax.shift_right_logical(cells, 8 + (SX * ngx).bit_length() - 1)
    row_x = place_x - gx * SX + TOP
    inside_x = (row_x >= 4) & (row_x < 28)
    nw = cells.shape[1]

    def spread(rows, row_of, lane_of, ok):
        at_row = lax.broadcasted_iota(jnp.int32, (rows, nw), 0)
        hot = jnp.where((at_row == row_of) & ok, 1.0, 0.0).astype(f32)
        at_lane = lax.broadcasted_iota(jnp.int32, (LY, nw), 0)
        val = jnp.where(at_lane == lane_of, rates[...], 0.0)
        return lax.dot_general(
            hot, val, (((1,), (1,)), ((), ())),
            precision=lax.Precision.HIGHEST, preferred_element_type=f32,
        )

    own_y = place_y - gy * LY
    well_main[...] = spread(
        NZ * EXT, place_z * EXT + row_x, own_y, inside_x & (own_y >= 0) & (own_y < LY)
    )
    col = place_y - (LY - 4)
    well_mini = spread(
        2 * EXT,
        lax.shift_right_logical(place_z, 4) * EXT + row_x,
        (place_z & 15) * 8 + col,
        inside_x & (col >= 0) & (col < 8),
    )

    def finish(flows, well):
        total = well + flows[0] + flows[1] + flows[2] + flows[3] + flows[4] + flows[5]
        total = jnp.where(total > 0, total, 1.0)
        scale = RELAX / total
        return total, [flow * scale for flow in flows]

    for zh in range(2):
        at = zh * EXT
        kx, ky, kz = (mfield[f, at : at + EXT, :] for f in range(3))
        other = mfield[2, (1 - zh) * EXT : (2 - zh) * EXT, :]
        xp = transmit(kx, pltpu.roll(kx, EXT - 1, 0))
        xm = pltpu.roll(xp, 1, 0)
        yp = transmit(ky, pltpu.roll(ky, LY - 1, 1))
        ym = pltpu.roll(yp, 1, 1)
        up = pltpu.roll(kz, LY - 8, 1)
        dn = pltpu.roll(kz, 8, 1)
        if zh == 0:
            up = jnp.where(lane < LY - 8, up, pltpu.roll(other, LY - 8, 1))
            zp = transmit(kz, up)
            zm = jnp.where(lane < 8, 0.0, transmit(kz, dn))
        else:
            dn = jnp.where(lane >= 8, dn, pltpu.roll(other, 8, 1))
            zp = jnp.where(lane < LY - 8, transmit(kz, up), 0.0)
            zm = transmit(kz, dn)
        unused, parts = finish((xm, xp, ym, yp, zm, zp), well_mini[at : at + EXT])
        for d in range(6):
            mcoef[d, at : at + EXT, :] = parts[d]

    def shift_of(z):
        return 123 + 2 * gy - 8 * (z & 15)

    def coefs(z, zm):
        base = pl.multiple_of(z * EXT, EXT)
        here = pl.ds(base, EXT)
        kx, ky, kz = (field[f, here, :] for f in range(3))
        half = pl.multiple_of(lax.shift_right_logical(z, 4) * EXT, EXT)
        edge = pltpu.roll(mfield[1, pl.ds(half, EXT), :], shift_of(z), 1)
        xp = transmit(kx, pltpu.roll(kx, EXT - 1, 0))
        xm = pltpu.roll(xp, 1, 0)
        yp = transmit(ky, jnp.where(lane == LY - 1, edge, pltpu.roll(ky, LY - 1, 1)))
        yp = jnp.where((lane == LY - 1) & (gy == 1), 0.0, yp)
        first = jnp.where(gy == 1, transmit(ky, edge), 0.0)
        ym = jnp.where(lane == 0, first, pltpu.roll(yp, 1, 1))
        later = pl.multiple_of(jnp.minimum(z + 1, NZ - 1) * EXT, EXT)
        zp = transmit(kz, field[2, pl.ds(later, EXT), :])
        zp = jnp.where(z == NZ - 1, 0.0, zp)
        total, parts = finish((xm, xp, ym, yp, zm, zp), well_main[here, :])
        diag[here, :] = total
        for d in range(6):
            coef[d, here, :] = parts[d]
        return zp

    lax.fori_loop(0, NZ, coefs, zero_tile)

    slot = lax.broadcasted_iota(jnp.int32, (SLOTS, LY), 0)
    slot_f = slot.astype(f32)
    bit = lax.shift_left(jnp.ones_like(slot), slot)
    lane8 = lax.broadcasted_iota(jnp.int32, (SLOTS, LY), 1)
    is_last = lane8 == LY - 1
    is_first = lane8 == 0
    zero8 = jnp.zeros((SLOTS, LY), f32)

    def wide(ref, row):
        return ref[pl.ds(row, SLOTS, stride=0), :]

    for zh in range(2):
        for s in range(RB):
            mbasis[0, zh, s] = (wide(mfield.at[3], zh * EXT + 4 + s) == slot_f).astype(f32)
    for it in range(ITERS):
        mbasis[it + 1] = jnp.zeros((2, RB, SLOTS, LY), f32)

        def window(s, carry):
            both = (mbasis[it, 0, s], mbasis[it, 1, s])
            ups = [pltpu.roll(v, LY - 8, 1) for v in both]
            dns = [pltpu.roll(v, 8, 1) for v in both]
            ups[0] = jnp.where(lane8 < LY - 8, ups[0], ups[1])
            dns[1] = jnp.where(lane8 >= 8, dns[1], dns[0])
            for zh in range(2):
                row = zh * EXT + 4 + s
                value = both[zh]
                near = (
                    mbasis[it, zh, s - 1], mbasis[it, zh, s + 1],
                    pltpu.roll(value, 1, 1), pltpu.roll(value, LY - 1, 1),
                    dns[zh], ups[zh],
                )
                new = (1.0 - RELAX) * value
                for d in range(6):
                    new = new + wide(mcoef.at[d], row) * near[d]
                bits = wide(mfield.at[4], row).astype(jnp.int32) & bit
                mbasis[it + 1, zh, s] = jnp.where(bits != 0, new, 0.0)
            return carry

        for s in range(it + 1, RB - it - 1):
            window(s, 0)

    for ref in (b0, b1):
        ref[0] = jnp.zeros((RB, SLOTS, LY), f32)
        ref[NZ + 1] = jnp.zeros((RB, SLOTS, LY), f32)

    def start(z, carry):
        for s in range(RB):
            b0[z + 1, s] = (wide(field.at[3], z * EXT + 4 + s) == slot_f).astype(f32)
        return carry

    lax.fori_loop(0, NZ, start, 0)

    def spread_sum(src, it, z, s, before, value, after):
        row = z * EXT + 4 + s
        edge = pltpu.roll(mbasis[it, lax.shift_right_logical(z, 4), s], shift_of(z), 1)
        left = jnp.where(is_first, edge, pltpu.roll(value, 1, 1))
        right = jnp.where(is_last, edge, pltpu.roll(value, LY - 1, 1))
        near = (before, after, left, right, src[z, s], src[z + 2, s])
        terms = [wide(coef.at[d], row) * near[d] for d in range(6)]
        return (terms[0] + terms[1]) + (terms[2] + terms[3]) + (terms[4] + terms[5])

    for it in range(ITERS):
        src, dst = ((b0, b1), (b1, b0))[it % 2]

        def smooth(z, carry):
            before = src[z + 1, it]
            value = src[z + 1, it + 1]
            for s in range(it + 1, RB - it - 1):
                after = src[z + 1, s + 1]
                new = (1.0 - RELAX) * value + spread_sum(src, it, z, s, before, value, after)
                bits = wide(ints, z * EXT + 4 + s) & bit
                dst[z + 1, s] = jnp.where(bits != 0, new, 0.0)
                before, value = value, after
            return carry

        lax.fori_loop(0, NZ, smooth, 0)

    src = (b0, b1)[ITERS % 2]
    acc[...] = jnp.zeros_like(acc)
    lhs[96:LY] = jnp.zeros((LY - 96, SX * LY), jnp.bfloat16)

    zero16 = jnp.zeros((2 * SLOTS, LY), jnp.bfloat16)

    def wide16(ref, row):
        one = wide(ref, row)
        return jnp.concatenate([one, one], 0).astype(jnp.bfloat16)

    def both_parts(value):
        high = value.astype(jnp.bfloat16).astype(f32)
        return high, value - high

    def gather(z, carry):
        before = src[z + 1, REACH - 1]
        value = src[z + 1, REACH]
        for x in range(SX):
            s = x + REACH
            after = src[z + 1, s + 1]
            total = spread_sum(src, ITERS, z, s, before, value, after)
            applied = wide(diag, z * EXT + 4 + s) * (value - 1.5 * total)
            out[pl.ds(z * SX + x, SLOTS, stride=NZ * SX), :] = value
            at = slice(x * LY, (x + 1) * LY)
            q = wide16(q_class, z * SX + x)
            y = wide16(y_class, z * SX + x)
            b16 = jnp.concatenate(both_parts(value), 0).astype(jnp.bfloat16)
            a16 = jnp.concatenate(both_parts(applied), 0).astype(jnp.bfloat16)
            for c in range(6):
                lhs[c * 16 : c * 16 + 16, at] = jnp.where(q == jnp.bfloat16(c), b16, zero16)
            for c in range(10):
                rhs[c * 16 : c * 16 + 16, at] = jnp.where(y == jnp.bfloat16(c), a16, zero16)
            before, value = value, after
        acc[...] += lax.dot_general(
            rhs[...], lhs[...], (((1,), (1,)), ((), ())), preferred_element_type=f32
        )
        return carry

    lax.fori_loop(0, NZ, gather, 0)


def body(conductivity, part_ids, support_mask, well_cells, well_rates):
    f32 = jnp.float32
    conductivity = conductivity.reshape(3, NZ * SX, LY)
    part_ids = part_ids.reshape(NZ * SX, LY)
    support_mask = support_mask.reshape(NZ * SX, LY)
    shape = jax.ShapeDtypeStruct
    mini, above, below, mini_y, mini_above, mini_below = pl.pallas_call(
        exchange_kernel,
        out_shape=(
            shape((5, 2, SX, LY), f32),
            shape((PLANES, NZ, LY), f32),
            shape((PLANES, NZ, LY), f32),
            shape((5, 2, SX, LY), f32),
            shape((5, 2, REACH, LY), f32),
            shape((5, 2, REACH, LY), f32),
        ),
        in_specs=[pl.BlockSpec(memory_space=pl.ANY)] * 3,
        out_specs=(VMEM,) * 6,
        scratch_shapes=[
            pltpu.VMEM((5, NZ * SX, LY), f32),
            pltpu.VMEM((NZ * SX, LY), jnp.int32),
            pltpu.VMEM((NZ * SX, LY), jnp.int32),
            pltpu.VMEM((PLANES, NZ, LY), f32),
            pltpu.VMEM((PLANES, NZ, LY), f32),
            pltpu.VMEM((5, 2, REACH, LY), f32),
            pltpu.VMEM((5, 2, REACH, LY), f32),
            pltpu.SemaphoreType.DMA((3,)),
            pltpu.SemaphoreType.DMA((5,)),
            pltpu.SemaphoreType.DMA((5,)),
        ],
        compiler_params=pltpu.CompilerParams(
            vmem_limit_bytes=60 * 2**20, collective_id=0, has_side_effects=True
        ),
        name="exchange",
    )(conductivity, part_ids, support_mask)
    basis, acc = pl.pallas_call(
        main_kernel,
        out_shape=(shape((SLOTS * NZ * SX, LY), f32), shape((160, LY), f32)),
        in_specs=[pl.BlockSpec(memory_space=pl.ANY)] * 3 + [VMEM] * 8,
        out_specs=(VMEM,) * 2,
        scratch_shapes=[
            pltpu.VMEM((5, NZ * EXT, LY), f32),
            pltpu.VMEM((6, NZ * EXT, LY), f32),
            pltpu.VMEM((NZ * EXT, LY), f32),
            pltpu.VMEM((NZ * EXT, LY), f32),
            pltpu.VMEM((NZ * SX, LY), f32),
            pltpu.VMEM((NZ * SX, LY), f32),
            pltpu.VMEM((NZ + 2, RB, SLOTS, LY), f32),
            pltpu.VMEM((NZ + 2, RB, SLOTS, LY), f32),
            pltpu.VMEM((5, 2 * EXT, LY), f32),
            pltpu.VMEM((6, 2 * EXT, LY), f32),
            pltpu.VMEM((ITERS + 1, 2, RB, SLOTS, LY), f32),
            pltpu.VMEM((LY, SX * LY), jnp.bfloat16),
            pltpu.VMEM((160, SX * LY), jnp.bfloat16),
            pltpu.VMEM((NZ * EXT, LY), jnp.int32),
            pltpu.VMEM((3, NZ * SX, LY), f32),
            pltpu.VMEM((NZ * SX, LY), jnp.int32),
            pltpu.VMEM((NZ * SX, LY), jnp.int32),
            pltpu.SemaphoreType.DMA((3,)),
        ],
        compiler_params=pltpu.CompilerParams(vmem_limit_bytes=60 * 2**20),
        name="smooth",
    )(
        conductivity, part_ids, support_mask, above, below, mini, mini_y, mini_above, mini_below,
        well_cells.reshape(1, -1), well_rates.reshape(1, -1),
    )
    sums = pl.pallas_call(
        total_kernel,
        out_shape=shape((64, LY), f32),
        in_specs=[VMEM],
        out_specs=VMEM,
        scratch_shapes=[
            pltpu.VMEM((80, LY), f32),
            pltpu.VMEM((8, LY), f32),
            pltpu.VMEM((80, LY), f32),
            pltpu.VMEM((80, LY), f32),
            pltpu.VMEM((8, LY), f32),
            pltpu.VMEM((8, LY), f32),
            pltpu.VMEM((8, LY), f32),
            pltpu.SemaphoreType.DMA((5,)),
            pltpu.SemaphoreType.DMA((5,)),
        ],
        compiler_params=pltpu.CompilerParams(collective_id=1, has_side_effects=True),
        name="total",
    )(acc)
    sums = sums[:, :32].reshape(8, SLOTS, 2, 2, SLOTS)[:, :, :, 0]
    total = jnp.transpose(sums, (0, 2, 3, 1))
    return (
        basis.reshape(SLOTS, NZ, SX, LY),
        total.reshape(1, 8, 2, SLOTS, SLOTS),
    )


def solution(mesh):
    placed = (
        P(None, "real", "gx", "gy"),
        P("real", "gx", "gy"),
        P("real", "gx", "gy"),
        P("real"),
        P("real"),
    )
    return jax.shard_map(
        body,
        mesh=mesh,
        in_specs=placed,
        out_specs=(P(None, "real", "gx", "gy"), P("gx", "gy", "real", None, None)),
        check_vma=False,
    )
```

```python
import jax
import jax.numpy as jnp
from jax import lax
from jax.experimental import pallas as pl
from jax.experimental.pallas import tpu as pltpu
from jax.sharding import PartitionSpec as P

NZ = 32
BLOCK = 16
SLOTS = 8
ITERS = 3
SX = 16
LY = 128
REACH = ITERS + 1
EXT = 32
TOP = 8
RB = SX + 2 * REACH
VMEM = pl.BlockSpec(memory_space=pltpu.VMEM)
RELAX = 2.0 / 3.0


def colour_of(ids):
    bx = lax.shift_right_logical(ids, 5)
    by = lax.shift_right_logical(ids, 1)
    return (bx & 1) * 4 + (by & 1) * 2 + (ids & 1)


def pack_window(get, rows):
    lane = lax.broadcasted_iota(jnp.int32, (rows, LY), 1)
    halves = []
    for zh in range(2):
        total = jnp.zeros((rows, LY), jnp.float32)
        for zl in range(16):
            moved = pltpu.roll(get(zh * 16 + zl), 8 * zl + 4, 1)
            total = jnp.where(lax.shift_right_logical(lane, 3) == zl, moved, total)
        halves.append(total)
    return halves


FROM_PREV = [
    (f, SX - REACH + i, TOP - REACH + i)
    for i in range(REACH)
    for f in ((0, 3) if i == 0 else range(5))
]
FROM_NEXT = [
    (f, i, TOP + SX + i) for i in range(REACH) for f in ((0, 3) if i == REACH - 1 else range(5))
]
PLANES = len(FROM_PREV)


def others(gx, gy, ngx):
    return (
        (gx < ngx - 1, {"gx": gx + 1, "gy": gy}),
        (gx > 0, {"gx": gx - 1, "gy": gy}),
        (None, {"gx": gx, "gy": 1 - gy}),
        (gx < ngx - 1, {"gx": gx + 1, "gy": 1 - gy}),
        (gx > 0, {"gx": gx - 1, "gy": 1 - gy}),
    )


def guarded(condition, action):
    if condition is None:
        action()
    else:
        pl.when(condition)(action)


def greet(targets):
    barrier = pltpu.get_barrier_semaphore()
    for condition, device in targets:
        guarded(condition, lambda: pl.semaphore_signal(
            barrier, inc=1, device_id=device, device_id_type=pl.DeviceIdType.MESH))
    ahead = jnp.minimum(lax.axis_size("gx") - 1 - lax.axis_index("gx"), 1)
    pl.semaphore_wait(barrier, 1 + 2 * ahead + 2 * jnp.minimum(lax.axis_index("gx"), 1))


def exchange_kernel(
    cond, part, mask, mini, above, below, mini_y, mini_above, mini_below,
    fields, part_in, mask_in, to_prev, to_next, mini_prev, mini_next, load_sem, send_sem, recv_sem,
):
    gx = lax.axis_index("gx")
    gy = lax.axis_index("gy")
    targets = others(gx, gy, lax.axis_size("gx"))
    loads = [
        pltpu.make_async_copy(cond, fields.at[0:3], load_sem.at[0]),
        pltpu.make_async_copy(part, part_in, load_sem.at[1]),
        pltpu.make_async_copy(mask, mask_in, load_sem.at[2]),
    ]
    for load in loads:
        load.start()
    has_source = (gx > 0, gx < lax.axis_size("gx") - 1)
    for ref, source in ((above, 0), (below, 1), (mini_above, 0), (mini_below, 1)):
        @pl.when(jnp.logical_not(has_source[source]))
        def _():
            ref[...] = jnp.zeros_like(ref)

    for load in loads:
        load.wait()
    fields[3] = colour_of(part_in[...]).astype(jnp.float32)
    fields[4] = mask_in[...].astype(jnp.float32)
    for n, (f, row, unused) in enumerate(FROM_NEXT):
        to_prev[n] = fields[f, pl.ds(row, NZ, stride=SX), :]
    for n, (f, row, unused) in enumerate(FROM_PREV):
        to_next[n] = fields[f, pl.ds(row, NZ, stride=SX), :]
    pairs = (
        (to_next, above), (to_prev, below), (mini, mini_y),
        (mini_next, mini_above), (mini_prev, mini_below),
    )
    copies = [
        pltpu.make_async_remote_copy(
            src_ref=src, dst_ref=dst, send_sem=send_sem.at[n], recv_sem=recv_sem.at[n],
            device_id=targets[n][1], device_id_type=pl.DeviceIdType.MESH,
        )
        for n, (src, dst) in enumerate(pairs)
    ]
    greet(targets)
    for n in (0, 1):
        guarded(targets[n][0], copies[n].start)
    for f in range(5):
        halves = pack_window(lambda z: fields[f, z * SX : z * SX + SX], SX)
        for zh in range(2):
            mini[f, zh] = halves[zh]
            mini_prev[f, zh] = halves[zh][0:REACH]
            mini_next[f, zh] = halves[zh][SX - REACH : SX]
    for n in (2, 3, 4):
        guarded(targets[n][0], copies[n].start)
    sources = (has_source[0], has_source[1], None, has_source[0], has_source[1])
    for n in range(5):
        guarded(targets[n][0], copies[n].wait_send)
        guarded(sources[n], copies[n].wait_recv)


def total_kernel(acc, out, grid, edge, from_prev, from_next, edge_y, edge_prev, edge_next,
                 send_sem, recv_sem):
    gx = lax.axis_index("gx")
    gy = lax.axis_index("gy")
    ngx = lax.axis_size("gx")
    targets = others(gx, gy, ngx)
    has_source = (gx > 0, gx < ngx - 1)
    for ref, source in ((from_prev, 0), (from_next, 1), (edge_prev, 0), (edge_next, 1)):
        @pl.when(jnp.logical_not(has_source[source]))
        def _():
            ref[...] = jnp.zeros_like(ref)

    for y in range(10):
        both = acc[y * 16 : y * 16 + 8] + acc[y * 16 + 8 : y * 16 + 16]
        grid[y * 8 : y * 8 + 8] = both + pltpu.roll(both, LY - 8, 1)
    edge[...] = jnp.where(gy == 1, grid[0:8], grid[72:80])
    pairs = ((grid, from_prev), (grid, from_next), (edge, edge_y), (edge, edge_prev), (edge, edge_next))
    copies = [
        pltpu.make_async_remote_copy(
            src_ref=src, dst_ref=dst, send_sem=send_sem.at[n], recv_sem=recv_sem.at[n],
            device_id=targets[n][1], device_id_type=pl.DeviceIdType.MESH,
        )
        for n, (src, dst) in enumerate(pairs)
    ]
    greet(targets)
    sources = (has_source[0], has_source[1], None, has_source[0], has_source[1])
    for n in range(5):
        guarded(targets[n][0], copies[n].start)
    for n in range(5):
        guarded(targets[n][0], copies[n].wait_send)
        guarded(sources[n], copies[n].wait_recv)
    for y in range(8):
        at = slice(y * 8 + 8, y * 8 + 16)
        mid, prev, after = grid[at], from_prev[at], from_next[at]
        if y in (0, 7):
            use = gy == (0 if y == 7 else 1)
            mid = mid + jnp.where(use, edge_y[...], 0.0)
            prev = prev + jnp.where(use, edge_prev[...], 0.0)
            after = after + jnp.where(use, edge_next[...], 0.0)
        out[y * 8 : y * 8 + 8] = (
            pltpu.roll(mid, LY - 32, 1) + after + pltpu.roll(prev, LY - 64, 1)
        )


def transmit(near, far):
    total = near + far
    good = total > 0
    return jnp.where(good, 2.0 * near * far / jnp.where(good, total, 1.0), 0.0)


def main_kernel(
    cond_hbm, part_hbm, mask_hbm, above, below, mini_own, mini_y, mini_above, mini_below, wells, rates,
    out, acc,
    field, coef, diag, well_main, q_class, y_class, b0, b1,
    mfield, mcoef, mbasis, lhs0, rhs0, lhs1, rhs1, turned, ints, cond, part, mask, load_sem,
):
    loads = [
        pltpu.make_async_copy(src, dst, load_sem.at[n])
        for n, (src, dst) in enumerate(((cond_hbm, cond), (part_hbm, part), (mask_hbm, mask)))
    ]
    for load in loads:
        load.start()
    for load in loads:
        load.wait()
    gx = lax.axis_index("gx")
    gy = lax.axis_index("gy")
    ngx = lax.axis_size("gx")
    f32 = jnp.float32
    lane = lax.broadcasted_iota(jnp.int32, (EXT, LY), 1)
    zero_tile = jnp.zeros((EXT, LY), f32)

    def fill(z, carry):
        base = pl.multiple_of(z * EXT, EXT)
        own = pl.multiple_of(z * EXT + TOP, 8)
        for f in range(5):
            field[f, pl.ds(base, 8), :] = zero_tile[:8]
            field[f, pl.ds(base + 24, 8), :] = zero_tile[:8]
        row = pl.multiple_of(z * SX, SX)
        ids = part[pl.ds(row, SX), :]
        for f in range(3):
            field[f, pl.ds(own, SX), :] = cond[f, pl.ds(row, SX), :]
        field[3, pl.ds(own, SX), :] = colour_of(ids).astype(f32)
        field[4, pl.ds(own, SX), :] = mask[pl.ds(row, SX), :].astype(f32)
        bx = lax.shift_right_logical(ids, 5) - gx + 1
        by = (lax.shift_right_logical(ids, 1) & 15) - gy * 8 + 1
        q_class[pl.ds(row, SX), :] = (bx * 2 + (ids & 1)).astype(f32)
        y_class[pl.ds(row, SX), :] = by.astype(f32)
        ints[pl.ds(base, 8), :] = jnp.zeros((8, LY), jnp.int32)
        ints[pl.ds(base + 24, 8), :] = jnp.zeros((8, LY), jnp.int32)
        ints[pl.ds(own, SX), :] = mask[pl.ds(row, SX), :]
        return carry

    lax.fori_loop(0, NZ, fill, 0, unroll=4)
    for planes, ref in ((FROM_PREV, above), (FROM_NEXT, below)):
        for n, (f, unused, row) in enumerate(planes):
            field[f, pl.ds(row, NZ, stride=EXT), :] = ref[n]
            if f == 4:
                ints[pl.ds(row, NZ, stride=EXT), :] = ref[n].astype(jnp.int32)

    side = lax.shift_right_logical(lane, 2) & 1
    for f in range(5):
        up = pack_window(lambda z: field[f, z * EXT + 4 : z * EXT + 8], REACH)
        dn = pack_window(lambda z: field[f, z * EXT + 24 : z * EXT + 28], REACH)
        for zh in range(2):
            at = zh * EXT
            mfield[f, at : at + 8, :] = zero_tile[:8]
            mfield[f, at + 24 : at + 32, :] = zero_tile[:8]
            mine4 = side[:REACH] == gy
            mfield[f, at + 4 : at + 8, :] = jnp.where(mine4, up[zh], mini_above[f, zh])
            mfield[f, at + 24 : at + 28, :] = jnp.where(mine4, dn[zh], mini_below[f, zh])
            mfield[f, at + 8 : at + 24, :] = jnp.where(
                side[:SX] == gy, mini_own[f, zh], mini_y[f, zh]
            )

    cells = wells[...]
    place_y = cells & 255
    place_x = lax.shift_right_logical(cells, 8) & (SX * ngx - 1)
    place_z = lax.shift_right_logical(cells, 8 + (SX * ngx).bit_length() - 1)
    row_x = place_x - gx * SX + TOP
    inside_x = (row_x >= 4) & (row_x < 28)
    nw = cells.shape[1]

    def spread(rows, row_of, lane_of, ok):
        at_row = lax.broadcasted_iota(jnp.int32, (rows, nw), 0)
        hot = jnp.where((at_row == row_of) & ok, 1.0, 0.0).astype(f32)
        at_lane = lax.broadcasted_iota(jnp.int32, (LY, nw), 0)
        val = jnp.where(at_lane == lane_of, rates[...], 0.0)
        return lax.dot_general(
            hot, val, (((1,), (1,)), ((), ())),
            precision=lax.Precision.HIGHEST, preferred_element_type=f32,
        )

    own_y = place_y - gy * LY
    well_main[...] = spread(
        NZ * EXT, place_z * EXT + row_x, own_y, inside_x & (own_y >= 0) & (own_y < LY)
    )
    col = place_y - (LY - 4)
    well_mini = spread(
        2 * EXT,
        lax.shift_right_logical(place_z, 4) * EXT + row_x,
        (place_z & 15) * 8 + col,
        inside_x & (col >= 0) & (col < 8),
    )

    def finish(flows, well):
        total = well + flows[0] + flows[1] + flows[2] + flows[3] + flows[4] + flows[5]
        total = jnp.where(total > 0, total, 1.0)
        scale = RELAX / total
        return total, [flow * scale for flow in flows]

    for zh in range(2):
        at = zh * EXT
        kx, ky, kz = (mfield[f, at : at + EXT, :] for f in range(3))
        other = mfield[2, (1 - zh) * EXT : (2 - zh) * EXT, :]
        xp = transmit(kx, pltpu.roll(kx, EXT - 1, 0))
        xm = pltpu.roll(xp, 1, 0)
        yp = transmit(ky, pltpu.roll(ky, LY - 1, 1))
        ym = pltpu.roll(yp, 1, 1)
        up = pltpu.roll(kz, LY - 8, 1)
        dn = pltpu.roll(kz, 8, 1)
        if zh == 0:
            up = jnp.where(lane < LY - 8, up, pltpu.roll(other, LY - 8, 1))
            zp = transmit(kz, up)
            zm = jnp.where(lane < 8, 0.0, transmit(kz, dn))
        else:
            dn = jnp.where(lane >= 8, dn, pltpu.roll(other, 8, 1))
            zp = jnp.where(lane < LY - 8, transmit(kz, up), 0.0)
            zm = transmit(kz, dn)
        unused, parts = finish((xm, xp, ym, yp, zm, zp), well_mini[at : at + EXT])
        for d in range(6):
            mcoef[d, at : at + EXT, :] = parts[d]

    def shift_of(z):
        return 123 + 2 * gy - 8 * (z & 15)

    def coefs(z, zm):
        base = pl.multiple_of(z * EXT, EXT)
        here = pl.ds(base, EXT)
        kx, ky, kz = (field[f, here, :] for f in range(3))
        half = pl.multiple_of(lax.shift_right_logical(z, 4) * EXT, EXT)
        edge = pltpu.roll(mfield[1, pl.ds(half, EXT), :], shift_of(z), 1)
        xp = transmit(kx, pltpu.roll(kx, EXT - 1, 0))
        xm = pltpu.roll(xp, 1, 0)
        yp = transmit(ky, jnp.where(lane == LY - 1, edge, pltpu.roll(ky, LY - 1, 1)))
        yp = jnp.where((lane == LY - 1) & (gy == 1), 0.0, yp)
        first = jnp.where(gy == 1, transmit(ky, edge), 0.0)
        ym = jnp.where(lane == 0, first, pltpu.roll(yp, 1, 1))
        later = pl.multiple_of(jnp.minimum(z + 1, NZ - 1) * EXT, EXT)
        zp = transmit(kz, field[2, pl.ds(later, EXT), :])
        zp = jnp.where(z == NZ - 1, 0.0, zp)
        total, parts = finish((xm, xp, ym, yp, zm, zp), well_main[here, :])
        diag[here, :] = total
        for d in range(6):
            coef[d, here, :] = parts[d]
        return zp

    lax.fori_loop(0, NZ, coefs, zero_tile, unroll=4)

    slot = lax.broadcasted_iota(jnp.int32, (SLOTS, LY), 0)
    slot_f = slot.astype(f32)
    bit = lax.shift_left(jnp.ones_like(slot), slot)
    lane8 = lax.broadcasted_iota(jnp.int32, (SLOTS, LY), 1)
    is_last = lane8 == LY - 1
    is_first = lane8 == 0
    zero8 = jnp.zeros((SLOTS, LY), f32)

    def wide(ref, row):
        return ref[pl.ds(row, SLOTS, stride=0), :]

    for zh in range(2):
        for s in range(RB):
            mbasis[0, zh, s] = (wide(mfield.at[3], zh * EXT + 4 + s) == slot_f).astype(f32)
    for it in range(ITERS):
        mbasis[it + 1] = jnp.zeros((2, RB, SLOTS, LY), f32)

        def window(s, carry):
            both = (mbasis[it, 0, s], mbasis[it, 1, s])
            ups = [pltpu.roll(v, LY - 8, 1) for v in both]
            dns = [pltpu.roll(v, 8, 1) for v in both]
            ups[0] = jnp.where(lane8 < LY - 8, ups[0], ups[1])
            dns[1] = jnp.where(lane8 >= 8, dns[1], dns[0])
            for zh in range(2):
                row = zh * EXT + 4 + s
                value = both[zh]
                near = (
                    mbasis[it, zh, s - 1], mbasis[it, zh, s + 1],
                    pltpu.roll(value, 1, 1), pltpu.roll(value, LY - 1, 1),
                    dns[zh], ups[zh],
                )
                new = (1.0 - RELAX) * value
                for d in range(6):
                    new = new + wide(mcoef.at[d], row) * near[d]
                bits = wide(mfield.at[4], row).astype(jnp.int32) & bit
                mbasis[it + 1, zh, s] = jnp.where(bits != 0, new, 0.0)
            return carry

        for s in range(it + 1, RB - it - 1):
            window(s, 0)

    for ref in (b0, b1):
        ref[0] = jnp.zeros((RB, SLOTS, LY), f32)
        ref[NZ + 1] = jnp.zeros((RB, SLOTS, LY), f32)

    def start(z, carry):
        for s in range(RB):
            b0[z + 1, s] = (wide(field.at[3], z * EXT + 4 + s) == slot_f).astype(f32)
        return carry

    lax.fori_loop(0, NZ, start, 0, unroll=2)

    def spread_sum(src, it, z, s, before, value, after):
        row = z * EXT + 4 + s
        edge = pltpu.roll(mbasis[it, lax.shift_right_logical(z, 4), s], shift_of(z), 1)
        left = jnp.where(is_first, edge, pltpu.roll(value, 1, 1))
        right = jnp.where(is_last, edge, pltpu.roll(value, LY - 1, 1))
        near = (before, after, left, right, src[z, s], src[z + 2, s])
        terms = [wide(coef.at[d], row) * near[d] for d in range(6)]
        return (terms[0] + terms[1]) + (terms[2] + terms[3]) + (terms[4] + terms[5])

    for it in range(ITERS):
        src, dst = ((b0, b1), (b1, b0))[it % 2]

        def smooth(z, carry):
            before = src[z + 1, it]
            value = src[z + 1, it + 1]
            for s in range(it + 1, RB - it - 1):
                after = src[z + 1, s + 1]
                new = (1.0 - RELAX) * value + spread_sum(src, it, z, s, before, value, after)
                bits = wide(ints, z * EXT + 4 + s) & bit
                dst[z + 1, s] = jnp.where(bits != 0, new, 0.0)
                before, value = value, after
            return carry

        lax.fori_loop(0, NZ, smooth, 0, unroll=4)

    src = (b0, b1)[ITERS % 2]
    acc[...] = jnp.zeros_like(acc)
    turned[...] = jnp.zeros_like(turned)
    lhs1[...] = jnp.zeros_like(lhs1)
    rhs1[...] = jnp.zeros_like(rhs1)

    def multiply(lhs, rhs):
        turned[...] += lax.dot_general(
            lhs[...], rhs[...], (((1,), (1,)), ((), ())), preferred_element_type=f32
        )


    zero16 = jnp.zeros((2 * SLOTS, LY), jnp.bfloat16)

    def wide16(ref, row):
        one = wide(ref, row)
        return jnp.concatenate([one, one], 0).astype(jnp.bfloat16)

    def both_parts(value):
        high = value.astype(jnp.bfloat16).astype(f32)
        return high, value - high

    def gather(z, lhs, rhs):
        before = src[z + 1, REACH - 1]
        value = src[z + 1, REACH]
        for x in range(SX):
            s = x + REACH
            after = src[z + 1, s + 1]
            total = spread_sum(src, ITERS, z, s, before, value, after)
            applied = wide(diag, z * EXT + 4 + s) * (value - 1.5 * total)
            out[pl.ds(z * SX + x, SLOTS, stride=NZ * SX), :] = value
            at = slice(x * LY, (x + 1) * LY)
            q = wide16(q_class, z * SX + x)
            y = wide16(y_class, z * SX + x)
            b16 = jnp.concatenate(both_parts(value), 0).astype(jnp.bfloat16)
            a16 = jnp.concatenate(both_parts(applied), 0).astype(jnp.bfloat16)
            for c in range(6):
                lhs[c * 16 : c * 16 + 16, at] = jnp.where(q == jnp.bfloat16(c), b16, zero16)
            for c in range(10):
                rhs[c * 16 : c * 16 + 16, at] = jnp.where(y == jnp.bfloat16(c), a16, zero16)
            before, value = value, after

    def gather_two(t, carry):
        multiply(lhs1, rhs1)
        gather(2 * t, lhs0, rhs0)
        multiply(lhs0, rhs0)
        gather(2 * t + 1, lhs1, rhs1)
        return carry

    lax.fori_loop(0, NZ // 2, gather_two, 0)
    multiply(lhs1, rhs1)
    acc[:, :96] = jnp.transpose(turned[...])


def body(conductivity, part_ids, support_mask, well_cells, well_rates):
    f32 = jnp.float32
    conductivity = conductivity.reshape(3, NZ * SX, LY)
    part_ids = part_ids.reshape(NZ * SX, LY)
    support_mask = support_mask.reshape(NZ * SX, LY)
    shape = jax.ShapeDtypeStruct
    mini, above, below, mini_y, mini_above, mini_below = pl.pallas_call(
        exchange_kernel,
        out_shape=(
            shape((5, 2, SX, LY), f32),
            shape((PLANES, NZ, LY), f32),
            shape((PLANES, NZ, LY), f32),
            shape((5, 2, SX, LY), f32),
            shape((5, 2, REACH, LY), f32),
            shape((5, 2, REACH, LY), f32),
        ),
        in_specs=[pl.BlockSpec(memory_space=pl.ANY)] * 3,
        out_specs=(VMEM,) * 6,
        scratch_shapes=[
            pltpu.VMEM((5, NZ * SX, LY), f32),
            pltpu.VMEM((NZ * SX, LY), jnp.int32),
            pltpu.VMEM((NZ * SX, LY), jnp.int32),
            pltpu.VMEM((PLANES, NZ, LY), f32),
            pltpu.VMEM((PLANES, NZ, LY), f32),
            pltpu.VMEM((5, 2, REACH, LY), f32),
            pltpu.VMEM((5, 2, REACH, LY), f32),
            pltpu.SemaphoreType.DMA((3,)),
            pltpu.SemaphoreType.DMA((5,)),
            pltpu.SemaphoreType.DMA((5,)),
        ],
        compiler_params=pltpu.CompilerParams(
            vmem_limit_bytes=60 * 2**20, collective_id=0, has_side_effects=True
        ),
        name="exchange",
    )(conductivity, part_ids, support_mask)
    basis, acc = pl.pallas_call(
        main_kernel,
        out_shape=(shape((SLOTS * NZ * SX, LY), f32), shape((160, LY), f32)),
        in_specs=[pl.BlockSpec(memory_space=pl.ANY)] * 3 + [VMEM] * 8,
        out_specs=(VMEM,) * 2,
        scratch_shapes=[
            pltpu.VMEM((5, NZ * EXT, LY), f32),
            pltpu.VMEM((6, NZ * EXT, LY), f32),
            pltpu.VMEM((NZ * EXT, LY), f32),
            pltpu.VMEM((NZ * EXT, LY), f32),
            pltpu.VMEM((NZ * SX, LY), f32),
            pltpu.VMEM((NZ * SX, LY), f32),
            pltpu.VMEM((NZ + 2, RB, SLOTS, LY), f32),
            pltpu.VMEM((NZ + 2, RB, SLOTS, LY), f32),
            pltpu.VMEM((5, 2 * EXT, LY), f32),
            pltpu.VMEM((6, 2 * EXT, LY), f32),
            pltpu.VMEM((ITERS + 1, 2, RB, SLOTS, LY), f32),
            pltpu.VMEM((96, SX * LY), jnp.bfloat16),
            pltpu.VMEM((160, SX * LY), jnp.bfloat16),
            pltpu.VMEM((96, SX * LY), jnp.bfloat16),
            pltpu.VMEM((160, SX * LY), jnp.bfloat16),
            pltpu.VMEM((96, 160), f32),
            pltpu.VMEM((NZ * EXT, LY), jnp.int32),
            pltpu.VMEM((3, NZ * SX, LY), f32),
            pltpu.VMEM((NZ * SX, LY), jnp.int32),
            pltpu.VMEM((NZ * SX, LY), jnp.int32),
            pltpu.SemaphoreType.DMA((3,)),
        ],
        compiler_params=pltpu.CompilerParams(vmem_limit_bytes=60 * 2**20),
        name="smooth",
    )(
        conductivity, part_ids, support_mask, above, below, mini, mini_y, mini_above, mini_below,
        well_cells.reshape(1, -1), well_rates.reshape(1, -1),
    )
    sums = pl.pallas_call(
        total_kernel,
        out_shape=shape((64, LY), f32),
        in_specs=[VMEM],
        out_specs=VMEM,
        scratch_shapes=[
            pltpu.VMEM((80, LY), f32),
            pltpu.VMEM((8, LY), f32),
            pltpu.VMEM((80, LY), f32),
            pltpu.VMEM((80, LY), f32),
            pltpu.VMEM((8, LY), f32),
            pltpu.VMEM((8, LY), f32),
            pltpu.VMEM((8, LY), f32),
            pltpu.SemaphoreType.DMA((5,)),
            pltpu.SemaphoreType.DMA((5,)),
        ],
        compiler_params=pltpu.CompilerParams(collective_id=1, has_side_effects=True),
        name="total",
    )(acc)
    sums = sums[:, :32].reshape(8, SLOTS, 2, 2, SLOTS)[:, :, :, 0]
    total = jnp.transpose(sums, (0, 2, 3, 1))
    return (
        basis.reshape(SLOTS, NZ, SX, LY),
        total.reshape(1, 8, 2, SLOTS, SLOTS),
    )


def solution(mesh):
    placed = (
        P(None, "real", "gx", "gy"),
        P("real", "gx", "gy"),
        P("real", "gx", "gy"),
        P("real"),
        P("real"),
    )
    return jax.shard_map(
        body,
        mesh=mesh,
        in_specs=placed,
        out_specs=(P(None, "real", "gx", "gy"), P("gx", "gy", "real", None, None)),
        check_vma=False,
    )
```
